256 devices in a mesh: cam: 64 (over z, y, core), rows: 4 (over x).
Axes of the slice: x: 4, y: 4, z: 8, core: 2. Of those that a mesh axis runs over, the one named last changes fastest.
Arguments:
- images: bfloat16 [64, 3, 32, 256], P('cam', None, 'rows'), may hold values from -6 to 6
- neighbor_ids: int32 [64, 6], P('cam'), may hold values from -1 to 63, as said below
- neighbor_count: int32 [64], P('cam'), may hold values from 2 to 6, as said below
- offsets: int32 [64, 6], P('cam'), may hold values from -1 to 1
- w_first: bfloat16 [64, 27], replicated, may hold values from -1.25 to 1.25
- w_second: bfloat16 [64, 64], replicated, may hold values from -0.75 to 0.75
- kernel_one: float32 [27], replicated, may hold values from -1.2 to 1.2
- kernel_two: float32 [27], replicated, may hold values from -1.2 to 1.2
- biases: float32 [2], replicated, may hold values from -0.6 to 0.6
Outputs:
- cost_volume: bfloat16 [64, 192, 32, 256], P('cam', None, 'rows')
The draws below stay inside these ranges and needn't reach their ends.
Inputs may be any that keep to these rules, and one draw needn't show every extreme that they name: For k < neighbor_count[i], neighbor_ids[i, k] is a camera at cycle distance 1 to 3 from camera i (modulo 64), no camera twice in one list; the remaining slots hold -1. `neighbor_count`: some camera has 6 neighbours and some has 2.
All inputs are finite; a program needn't handle non-finite values.
Results may differ from the reference program's by a relative error of at most 0.012.
Values may be sent and summed in bfloat16 or wider, within the bound.
No kernel may reach another device: no remote copies, remote signals or barrier semaphores. Data moves between devices by JAX's collectives and lax.ppermute only.
A program may use at most 128 MiB of HBM per device.

```python
import jax
import jax.numpy as jnp
from jax import lax

C = 64
D = 192
W = 256
REACH = 3
NBR = 6
CAMS = 64
H = 32


def pair_lists(key):
    count_key = jax.random.fold_in(key, 101)
    numbers = jax.random.randint(count_key, (CAMS,), 2, NBR + 1)
    shuffled = jax.random.permutation(jax.random.fold_in(key, 102), CAMS)
    numbers = numbers.at[shuffled[0]].set(NBR).at[shuffled[1]].set(2)
    columns = jnp.arange(NBR, dtype=jnp.int32)
    scores = jax.random.randint(jax.random.fold_in(key, 103), (CAMS, NBR), 0, 1000) * NBR + columns[None, :]
    ranking = jnp.argsort(scores, axis=1)
    distances = jnp.where(columns < REACH, columns - REACH, columns - REACH + 1)
    chosen = distances[ranking]
    cameras = (jnp.arange(CAMS, dtype=jnp.int32)[:, None] + chosen) % CAMS
    listed = jnp.where(columns[None, :] < numbers[:, None], cameras, -1)
    return (numbers.astype(jnp.int32), listed.astype(jnp.int32))


def draw_neighbor_ids(key, part):
    numbers, listed = pair_lists(key)
    return listed


def draw_neighbor_count(key, part):
    numbers, listed = pair_lists(key)
    return numbers


def touch_ends(array, own_key, low, high):
    longest = array.shape.index(max(array.shape))
    spots = []
    for shift in (0, 1):
        where = [jax.random.randint(jax.random.fold_in(own_key, axis), (), 0, length) for axis, length in enumerate(array.shape)]
        where[longest] = (where[longest] + shift) % array.shape[longest]
        spots.append(tuple(where))
    return array.at[spots[0]].set(low).at[spots[1]].set(high)


def shard_levels(own_key, dims, shards, smallest, top_value):
    gain, own = 1.0, jax.random.fold_in(own_key, 6)
    for dim, parts in shards:
        draws = jnp.exp(jax.random.uniform(jax.random.fold_in(own, dim), (parts,), jnp.float32, smallest / len(shards), top_value / len(shards)))
        gain = gain * jnp.repeat(draws, dims[dim] // parts).reshape([-1 if axis == dim else 1 for axis in range(len(dims))])
    return gain


def bell_draw(own_key, dims, scale, most, cuts=(), kind=jnp.bfloat16):
    values = jax.random.normal(own_key, dims, jnp.float32) * scale
    if len(cuts) > 0:
        values = shard_levels(own_key, dims, cuts, -0.22, 0.18) * values
    return jnp.clip(values, min=-most, max=most).astype(kind)


def setup_inputs(seed: int = 0) -> dict:
    seeds = jax.random.split(jax.random.key(seed), 10)
    return {
        "images": bell_draw(seeds[0], (CAMS, 3, H, W), 1.0, 6.0, ((0, 64), (2, 4))),
        "neighbor_ids": draw_neighbor_ids(jax.random.fold_in(seeds[9], 71), 0),
        "neighbor_count": draw_neighbor_count(jax.random.fold_in(seeds[9], 71), 0),
        "offsets": touch_ends(jax.random.randint(seeds[3], (CAMS, NBR), -1, 2), jax.random.fold_in(seeds[3], 1), -1, 1).astype(jnp.int32),
        "w_first": bell_draw(seeds[4], (C, 27), 27 ** -0.5, 1.25),
        "w_second": bell_draw(seeds[5], (C, C), C ** -0.5, 0.75),
        "kernel_one": bell_draw(seeds[6], (27,), 0.3, 1.2, (), jnp.float32),
        "kernel_two": bell_draw(seeds[7], (27,), 0.3, 1.2, (), jnp.float32),
        "biases": jnp.clip(jax.random.uniform(seeds[8], (2,), jnp.float32, -0.6, 0.6), -0.6, 0.6),
    }


def features_of(image_rows, w_first, w_second):
    rows_out = image_rows.shape[1] - 2
    width = image_rows.shape[2]
    padded = jnp.pad(image_rows, ((0, 0), (0, 0), (1, 1)))
    patches = jnp.stack([padded[plane, tap_row:tap_row + rows_out, tap_col:tap_col + width] for plane in range(3) for tap_row in range(3) for tap_col in range(3)])
    hidden = jnp.einsum('ok,kyx->oyx', w_first.astype(jnp.float32), patches.astype(jnp.float32))
    hidden = jax.nn.relu(hidden).astype(jnp.bfloat16)
    mapped = jnp.einsum('oc,cyx->oyx', w_second.astype(jnp.float32), hidden.astype(jnp.float32))
    return mapped.astype(jnp.bfloat16)

def correlate(left_feats, right_feats):
    channels, count_rows, width = left_feats.shape
    tile = 128 if width % 128 == 0 else width
    tiles = width // tile
    span = tile + D - 1
    padded = jnp.pad(right_feats, ((0, 0), (0, 0), (D, 0)))
    windows = jnp.stack([padded[:, :, start + 1:start + 1 + span] for start in range(0, width, tile)], axis=2)
    blocks = left_feats.reshape(channels, count_rows, tiles, tile)
    products = jnp.einsum('cpti,cptl->ptil', blocks.astype(jnp.float32), windows.astype(jnp.float32))
    flat = products.reshape(count_rows, tiles, tile * span)
    flat = jnp.pad(flat, ((0, 0), (0, 0), (0, tile)))
    skewed = flat.reshape(count_rows, tiles, tile, tile + D)[:, :, :, :D]
    result = skewed.transpose(3, 0, 1, 2).reshape(D, count_rows, width)
    return result * (1.0 / jnp.sqrt(jnp.float32(channels)))

def filter_three(volume_rows, kernel):
    depth, count_rows, width = volume_rows.shape
    rows_out = count_rows - 2
    padded = jnp.pad(volume_rows, ((1, 1), (0, 0), (1, 1))).astype(jnp.float32)
    total = jnp.zeros((depth, rows_out, width), jnp.float32)
    for tap_d in range(3):
        for tap_row in range(3):
            for tap_col in range(3):
                total = total + kernel[9 * tap_d + 3 * tap_row + tap_col] * padded[tap_d:tap_d + depth, tap_row:tap_row + rows_out, tap_col:tap_col + width]
    return total

def reference(images, neighbor_ids, neighbor_count, offsets, w_first, w_second, kernel_one, kernel_two, biases):
    all_feats = lax.map(lambda picture: features_of(jnp.pad(picture, ((0, 0), (1, 1), (0, 0))), w_first, w_second), images)

    def one_camera(camera):
        own_feats = lax.dynamic_index_in_dim(all_feats, camera, 0, keepdims=False)
        listed = lax.dynamic_index_in_dim(neighbor_ids, camera, 0, keepdims=False)
        shifts = lax.dynamic_index_in_dim(offsets, camera, 0, keepdims=False)
        number = lax.dynamic_index_in_dim(neighbor_count, camera, 0, keepdims=False)
        summed = jnp.zeros((D, H, W), jnp.float32)
        for slot in range(NBR):
            other = jnp.maximum(listed[slot], 0).astype(jnp.int32)
            other_feats = lax.dynamic_index_in_dim(all_feats, other, 0, keepdims=False)
            other_feats = jnp.pad(other_feats, ((0, 0), (1, 1), (0, 0)))
            other_feats = lax.dynamic_slice_in_dim(other_feats, (1 + shifts[slot]).astype(jnp.int32), H, 1)
            summed = summed + jnp.where(slot < number, jax.nn.relu(correlate(own_feats, other_feats)), jnp.float32(0.0))
        volume = (summed / number.astype(jnp.float32)).astype(jnp.bfloat16)
        smoothed = jax.nn.relu(filter_three(jnp.pad(volume, ((0, 0), (1, 1), (0, 0))), kernel_one) + biases[0]).astype(jnp.bfloat16)
        return (filter_three(jnp.pad(smoothed, ((0, 0), (1, 1), (0, 0))), kernel_two) + biases[1]).astype(jnp.bfloat16)
    return lax.map(one_camera, jnp.arange(CAMS, dtype=jnp.int32))
```

```python
import jax
import jax.numpy as jnp
import numpy as np
from jax import lax
from jax.experimental import pallas as pl
from jax.experimental.pallas import tpu as pltpu
from jax.sharding import PartitionSpec as P

C = 64
D = 192
W = 256
NBR = 6
CAMS = 64
H = 32
BAND = 8
ROWS = BAND + 4
TALL = BAND + 8
TAPS = 9 * TALL
DISTANCES = (-3, -2, -1, 1, 2, 3)
BLOCKS = D // 8
F32 = jnp.float32
BF16 = jnp.bfloat16


def spread_of_taps():
    spread = np.zeros((27, ROWS, 256), np.float32)
    for y in range(ROWS):
        for p in range(3):
            for a in range(3):
                for b in range(3):
                    spread[9 * p + 3 * a + b, y, (3 * p + b) * TALL + y + a + 1] = 1.0
    return spread.reshape(27, ROWS * 256)


def iota(shape, axis):
    return lax.broadcasted_iota(jnp.int32, shape, axis)


def fill_taps(a, b, e, taps_ref):
    ok = (a >= 0) & (a <= 2) & (b >= 0) & (b <= 2)
    code = jnp.where(ok, 9 * a + 3 * b + e, 27)
    filled = jnp.zeros(code.shape, F32)
    for tap in range(27):
        filled = jnp.where(code == tap, taps_ref[tap], filled)
    high = filled.astype(BF16)
    return high, (filled - high.astype(F32)).astype(BF16)


def prepare_kernel(w_first, spread, k_one, k_two, wide, one, two):
    taps = jnp.dot(w_first[...], spread[...], preferred_element_type=F32).astype(BF16)
    for y in range(ROWS):
        wide[64 * y : 64 * y + 64, :] = taps[:, 256 * y : 256 * y + TAPS]
    shape = (120, 192)
    m, k = iota(shape, 0), iota(shape, 1)
    q = m >> 3
    e = (q >= 5).astype(jnp.int32) + (q >= 10).astype(jnp.int32)
    a = 8 * (k >> 6) - 7 + (k & 7) - (m & 7)
    b = ((k >> 3) & 7) - (q - 5 * e)
    for half in range(2):
        one[half, 0], one[half, 1] = fill_taps(a, b - half, e, k_one)
    shape = (192, 240)
    m, k = iota(shape, 0), iota(shape, 1)
    q = k >> 3
    t = (q >= 10).astype(jnp.int32) + (q >= 20).astype(jnp.int32)
    a = 8 * t - 7 + (k & 7) - ((m >> 3) & 7)
    b = (q - 10 * t) - (m & 7)
    two[0], two[1] = fill_taps(a, b, m >> 6, k_two)


def prepare(w_first, kernel_one, kernel_two):
    spread = jnp.asarray(spread_of_taps(), BF16)
    vmem, smem = pl.BlockSpec(memory_space=pltpu.VMEM), pl.BlockSpec(memory_space=pltpu.SMEM)
    return pl.pallas_call(
        prepare_kernel,
        out_shape=(
            jax.ShapeDtypeStruct((64 * ROWS, TAPS), BF16),
            jax.ShapeDtypeStruct((2, 2, 120, 192), BF16),
            jax.ShapeDtypeStruct((2, 192, 240), BF16),
        ),
        in_specs=[vmem, vmem, smem, smem],
        out_specs=(vmem, vmem, vmem),
        name="prepare",
        cost_estimate=pl.CostEstimate(flops=3000000, bytes_accessed=1000000, transcendentals=0),
        compiler_params=pltpu.CompilerParams(vmem_limit_bytes=32 * 1024 * 1024),
    )(w_first, spread, kernel_one, kernel_two)


def turned_columns(value):
    mirror = (iota((W, W), 0) + iota((W, W), 1) == W - 1).astype(F32).astype(BF16)
    return jnp.dot(value, mirror, preferred_element_type=F32)


def columns_of(picture_of, shift):
    lane = iota((TALL, W), 1)
    parts = []
    for p in range(3):
        rows = picture_of(p).astype(F32)
        if shift is not None:
            rows = pltpu.roll(rows, jnp.where(shift > 0, TALL - shift, -shift), axis=0)
        sides = [
            jnp.where(lane == 0, 0.0, pltpu.roll(rows, 1, axis=1)),
            rows,
            jnp.where(lane == W - 1, 0.0, pltpu.roll(rows, W - 1, axis=1)),
        ]
        parts += sides if shift is None else sides[::-1]
    return jnp.concatenate(parts, axis=0).astype(BF16)


def side_sum(parts):
    lane = iota(parts[0].shape, 1)
    left = jnp.where(lane == 0, 0.0, pltpu.roll(parts[0], 1, axis=1))
    right = jnp.where(lane == W - 1, 0.0, pltpu.roll(parts[2], W - 1, axis=1))
    return left + parts[1] + right


def main_kernel(
    place, ids, count, offsets, biases, pictures, w_second, wide, one, two, out, right, left, vol, smooth
):
    camera, first = place[0], place[1]
    number = count[0]

    def features(columns, group, shift, listed):
        hidden = jnp.dot(wide[256 * group : 256 * group + 256, :], columns, preferred_element_type=F32)
        found = []
        for q in range(4):
            row = first - 2 + 4 * group + q + shift
            keep = jnp.where((row >= 0) & (row < H) & listed, 1.0, 0.0)
            part = jnp.maximum(hidden[64 * q : 64 * q + 64], 0.0) * keep
            found.append(jnp.dot(w_second[...], part.astype(BF16), preferred_element_type=F32))
        return found

    columns = columns_of(lambda p: pictures[0, p], None)
    lane = iota((W, 128), 1)
    for group in range(3):
        found = features(columns, group, 0, True)
        for half in range(2):
            pair = jnp.concatenate(found[2 * half : 2 * half + 2], axis=0).T
            left[2 * group + half, 0:W] = jnp.where(lane < 64, pair, 0.0).astype(BF16)
            left[2 * group + half, W : 2 * W] = jnp.where(lane >= 64, pair, 0.0).astype(BF16)

    mirrored = turned_columns(pictures[1 : NBR + 1].reshape(3 * NBR * TALL, W))
    for index, distance in enumerate(DISTANCES):
        other = (camera + distance + CAMS) & (CAMS - 1)
        shift, listed = jnp.int32(0), jnp.bool_(False)
        for slot in range(NBR):
            here = (ids[0, slot] == other) & (slot < number)
            shift = jnp.where(here, offsets[0, slot], shift)
            listed = listed | here
        columns = columns_of(
            lambda p: mirrored[(3 * index + p) * TALL : (3 * index + p + 1) * TALL], shift
        )
        for group in range(3):
            for q, part in enumerate(features(columns, group, shift, listed)):
                at = 256 * group + 64 * q
                right[index, at : at + 64] = part.astype(BF16)

    zero = jnp.zeros((96, W), BF16)
    vol[0] = zero
    vol[BLOCKS + 1] = zero
    smooth[0] = zero[:80]
    smooth[BLOCKS + 1] = zero[:80]

    scale = jnp.float32(1.0 / 8 / 6)
    for n in range(2, 6):
        scale = jnp.where(number == n, jnp.float32(1.0 / 8 / n), scale)
    swap = (iota((D, W), 0) + iota((D, W), 1) == D - 1).astype(F32).astype(BF16)
    inside = iota((128, 128), 0) + iota((128, 128), 1) >= 127

    def pair_rows(pair, carry):
        done = []
        for one_row in range(2):
            top = left[pair, 256 * one_row : 256 * one_row + 128]
            bottom = left[pair, 256 * one_row + 128 : 256 * one_row + 256]
            upper = lower = None
            for index in range(NBR):
                other = right[index, pl.ds(pl.multiple_of(128 * pair, 128), 128), :]
                a = jnp.maximum(jnp.dot(top, other[:, 128:], preferred_element_type=F32), 0.0)
                b = jnp.maximum(jnp.dot(bottom, other, preferred_element_type=F32), 0.0)
                upper = a if upper is None else upper + a
                lower = b if lower is None else lower + b
            upper = jnp.where(inside, upper * scale, 0.0)
            lower = lower * scale
            summed = jnp.concatenate(
                [
                    jnp.concatenate([jnp.zeros((128, 128), F32), upper], axis=1),
                    jnp.concatenate([jnp.where(inside, lower[:, :128], 0.0), lower[:, 128:]], axis=1),
                ],
                axis=0,
            )
            turned = pltpu.roll(summed, 1, axis=1, stride=1, stride_axis=0).astype(BF16)
            flipped = lax.dot_general(
                swap, turned, (((1,), (1,)), ((), ())), preferred_element_type=F32
            )
            done.append(flipped.reshape(BLOCKS, 8, W))
        both = jnp.concatenate(done, axis=1).astype(BF16)
        vol[1 : BLOCKS + 1, pl.ds(pl.multiple_of(16 * pair, 16), 16), :] = both
        return carry

    lax.fori_loop(0, ROWS // 2, pair_rows, 0)

    bias_one, bias_two = biases[0], biases[1]
    above_ok = jnp.where(first > 0, 1.0, 0.0)
    under_ok = jnp.where(first + BAND < H, 1.0, 0.0)

    def first_filter(block, carry):
        halves = []
        for half in range(2):
            source = vol[pl.ds(block, 3), 32 * half : 32 * half + 64, :].reshape(192, W)
            total = jnp.dot(one[half, 0], source, preferred_element_type=F32)
            total = total + jnp.dot(one[half, 1], source, preferred_element_type=F32)
            halves.append(side_sum([total[40 * e : 40 * e + 40] for e in range(3)]))
        result = jnp.maximum(jnp.concatenate(halves, axis=0) + bias_one, 0.0)
        result = jnp.concatenate(
            [result[:8] * above_ok, result[8:72], result[72:] * under_ok], axis=0
        )
        smooth[block + 1] = result.astype(BF16)
        return carry

    lax.fori_loop(0, BLOCKS, first_filter, 0)

    def second_filter(block, carry):
        source = smooth[pl.ds(block, 3)].reshape(240, W)
        total = jnp.dot(two[0], source, preferred_element_type=F32)
        total = total + jnp.dot(two[1], source, preferred_element_type=F32)
        result = side_sum([total[64 * e : 64 * e + 64] for e in range(3)]) + bias_two
        out[0, pl.ds(8 * block, 8)] = result.reshape(8, BAND, W).astype(BF16)
        return carry

    lax.fori_loop(0, BLOCKS, second_filter, 0)


def cost_volume(place, ids, count, offsets, biases, pictures, w_second, wide, one, two):
    vmem, smem = pl.BlockSpec(memory_space=pltpu.VMEM), pl.BlockSpec(memory_space=pltpu.SMEM)
    return pl.pallas_call(
        main_kernel,
        out_shape=jax.ShapeDtypeStruct((1, D, BAND, W), BF16),
        in_specs=[smem] * 5 + [vmem] * 5,
        out_specs=vmem,
        scratch_shapes=[
            pltpu.VMEM((NBR, 64 * ROWS, W), BF16),
            pltpu.VMEM((ROWS // 2, 2 * W, 128), BF16),
            pltpu.VMEM((BLOCKS + 2, 8 * ROWS, W), BF16),
            pltpu.VMEM((BLOCKS + 2, 8 * (BAND + 2), W), BF16),
        ],
        name="cost_volume",
        cost_estimate=pl.CostEstimate(flops=20000000000, bytes_accessed=3000000, transcendentals=0),
        compiler_params=pltpu.CompilerParams(vmem_limit_bytes=48 * 1024 * 1024),
    )(place, ids, count, offsets, biases, pictures, w_second, wide, one, two)


def from_camera(value, distance):
    pairs = [((to + distance) % CAMS, to) for to in range(CAMS)]
    return lax.ppermute(value, "cam", pairs)


def on_device(
    images, neighbor_ids, neighbor_count, offsets, w_first, w_second, kernel_one, kernel_two, biases
):
    ends = lax.axis_size("rows") - 1
    over = lax.ppermute(images, "rows", [(i, i + 1) for i in range(ends)])
    under = lax.ppermute(images, "rows", [(i + 1, i) for i in range(ends)])
    own = jnp.concatenate([over[:, :, 4:], images, under[:, :, :4]], axis=2)
    wide, one, two = prepare(w_first, kernel_one, kernel_two)
    pictures = jnp.concatenate([own] + [from_camera(own, d) for d in DISTANCES], axis=0)
    place = jnp.stack([lax.axis_index("cam"), lax.axis_index("rows") * BAND]).astype(jnp.int32)
    return cost_volume(
        place, neighbor_ids, neighbor_count, offsets, biases, pictures, w_second, wide, one, two
    )


def solution(mesh):
    in_specs = (
        P("cam", None, "rows", None),
        P("cam", None),
        P("cam"),
        P("cam", None),
        P(),
        P(),
        P(),
        P(),
        P(),
    )
    out_specs = P("cam", None, "rows", None)
    return jax.shard_map(
        on_device, mesh=mesh, in_specs=in_specs, out_specs=out_specs, check_vma=False
    )
```

```python
import jax
import jax.numpy as jnp
from jax import lax
from jax.experimental import pallas as pl
from jax.experimental.pallas import tpu as pltpu
from jax.sharding import PartitionSpec as P

C = 64
D = 192
W = 256
NBR = 6
CAMS = 64
H = 32
BAND = 8
ROWS = BAND + 4
TALL = BAND + 8
TAPS = 9 * TALL
BLOCKS = D // 8
F32 = jnp.float32
BF16 = jnp.bfloat16


def iota(shape, axis):
    return lax.broadcasted_iota(jnp.int32, shape, axis)


def one_hot(condition):
    return condition.astype(F32).astype(BF16)


def spread_first(w_first, wide):
    shape = (27, 256)
    tap, k = iota(shape, 0), iota(shape, 1)
    q = k >> 4
    p = (q * 11) >> 5
    for y in range(ROWS):
        a = (k & 15) - y - 1
        chosen = (a >= 0) & (a <= 2) & (q < 9) & (tap == 6 * p + q + 3 * a)
        taps = transposed_dot(w_first[...], one_hot(chosen))
        wide[64 * y : 64 * y + 64, :] = taps[:, :TAPS].astype(BF16)


def fill_taps(a, b, taps_ref, store):
    masks = [[(a == i) & (b == j) for j in range(3)] for i in range(3)]
    for e in range(3):
        filled = jnp.zeros(a.shape, F32)
        for i in range(3):
            for j in range(3):
                filled = jnp.where(masks[i][j], taps_ref[9 * i + 3 * j + e], filled)
        high = filled.astype(BF16)
        store(e, high, (filled - high.astype(F32)).astype(BF16))


def spread_filters(k_one, k_two, one, two):
    shape = (40, 192)
    m, k = iota(shape, 0), iota(shape, 1)
    a = 8 * (k >> 6) - 7 + (k & 7) - (m & 7)
    b = ((k >> 3) & 7) - (m >> 3)
    for half in range(2):
        parts = [[], []]

        def keep(e, high, low):
            parts[0].append(high.astype(F32))
            parts[1].append(low.astype(F32))

        fill_taps(a, b - half, k_one, keep)
        for n in range(2):
            one[half, n] = jnp.concatenate(parts[n], axis=0).astype(BF16)
    shape = (64, 240)
    m, k = iota(shape, 0), iota(shape, 1)
    q = k >> 3
    t = (q >= 10).astype(jnp.int32) + (q >= 20).astype(jnp.int32)
    a = 8 * t - 7 + (k & 7) - (m >> 3)
    b = (q - 10 * t) - (m & 7)

    def save(e, high, low):
        two[0, 64 * e : 64 * e + 64] = high
        two[1, 64 * e : 64 * e + 64] = low

    fill_taps(a, b, k_two, save)


def turned_columns(value):
    mirror = one_hot(iota((W, W), 0) + iota((W, W), 1) == W - 1)
    return jnp.dot(value, mirror, preferred_element_type=F32)


def columns_of(picture_of, shift):
    lane = iota((TALL, W), 1)
    parts = []
    for p in range(3):
        rows = picture_of(p).astype(F32)
        if shift is not None:
            rows = pltpu.roll(rows, jnp.where(shift > 0, TALL - shift, -shift), axis=0)
        sides = [
            jnp.where(lane == 0, 0.0, pltpu.roll(rows, 1, axis=1)),
            rows,
            jnp.where(lane == W - 1, 0.0, pltpu.roll(rows, W - 1, axis=1)),
        ]
        parts += sides if shift is None else sides[::-1]
    return jnp.concatenate(parts, axis=0).astype(BF16)


def side_sum(parts):
    lane = iota(parts[0].shape, 1)
    left = jnp.where(lane == 0, 0.0, pltpu.roll(parts[0], 1, axis=1))
    right = jnp.where(lane == W - 1, 0.0, pltpu.roll(parts[2], W - 1, axis=1))
    return left + parts[1] + right


def transposed_dot(first, second):
    return lax.dot_general(first, second, (((0,), (0,)), ((), ())), preferred_element_type=F32)


def features(columns, wide, w_second, group, top, listed):
    hidden = jnp.dot(wide[256 * group : 256 * group + 256, :], columns, preferred_element_type=F32)
    found = []
    for q in range(4):
        row = top + 4 * group + q
        keep = jnp.where((row >= 0) & (row < H) & listed, 1.0, 0.0)
        part = jnp.maximum(hidden[64 * q : 64 * q + 64], 0.0) * keep
        found.append(jnp.dot(w_second[...], part.astype(BF16), preferred_element_type=F32))
    return found


def read_table(table):
    value = [table[n] for n in range(15)]
    return value[0:2], value[2:8], value[14:15], value[8:14]


def wrapped(camera):
    return (camera + CAMS) & (CAMS - 1)


def neighbour_features(others, pictures, wide, w_second, place, ids, count, offsets, right):
    number = len(others)
    mirrored = turned_columns(pictures.reshape(number * 3 * TALL, W))
    for index, other in enumerate(others):
        shift, listed = jnp.int32(0), jnp.bool_(False)
        for slot in range(NBR):
            here = (ids[slot] == other) & (slot < count[0])
            shift = jnp.where(here, offsets[slot], shift)
            listed = listed | here
        columns = columns_of(
            lambda p: mirrored[(3 * index + p) * TALL : (3 * index + p + 1) * TALL], shift
        )
        for group in range(3):
            parts = features(columns, wide, w_second, group, place[1] - 2 + shift, listed)
            for q, part in enumerate(parts):
                at = 256 * group + 64 * q
                right[index, at : at + 64] = part.astype(BF16)


def correlated(left, right, row, upper, lower):
    pair, base = row // 2, W * (row % 2)
    top = left[pair, base : base + 128]
    bottom = left[pair, base + 128 : base + 256]
    for index in range(right.shape[0]):
        other = right[index, 128 * pair : 128 * pair + 128, :]
        a = jnp.maximum(jnp.dot(top, other[:, 128:], preferred_element_type=F32), 0.0)
        b = jnp.maximum(jnp.dot(bottom, other, preferred_element_type=F32), 0.0)
        upper = a if upper is None else upper + a
        lower = b if lower is None else lower + b
    return upper, lower


def early_kernel(table, w_first, w_second, pictures, left, upper, lower, wide, right, sems, first_w, second_w):
    place, ids, count, offsets = read_table(table)
    loads = [
        pltpu.make_async_copy(w_first, first_w, sems.at[0]),
        pltpu.make_async_copy(w_second, second_w, sems.at[1]),
    ]
    for load in loads:
        load.start()
    for load in loads:
        load.wait()
    w_first, w_second = first_w, second_w
    spread_first(w_first, wide)
    columns = columns_of(lambda p: pictures[0, p], None)
    lane = iota((W, 128), 1)
    for group in range(3):
        found = features(columns, wide, w_second, group, place[1] - 2, True)
        for half in range(2):
            pair = jnp.concatenate(found[2 * half : 2 * half + 2], axis=0).T
            left[2 * group + half, 0:W] = jnp.where(lane < 64, pair, 0.0).astype(BF16)
            left[2 * group + half, W : 2 * W] = jnp.where(lane >= 64, pair, 0.0).astype(BF16)
    neighbour_features(
        [place[0] ^ 1], pictures[1], wide, w_second, place, ids, count, offsets, right
    )
    for row in range(ROWS):
        upper[row], lower[row] = correlated(left, right, row, None, None)


def late_kernel(
    table, floats, w_first, w_second, pictures, left, upper_sum, lower_sum,
    out, wide, one, two, right, vol, smooth, sems, first_w, second_w,
):
    loads = [
        pltpu.make_async_copy(w_first, first_w, sems.at[0]),
        pltpu.make_async_copy(w_second, second_w, sems.at[1]),
    ]
    for load in loads:
        load.start()
    place, ids, count, offsets = read_table(table)
    k_one = [floats[n] for n in range(27)]
    k_two = [floats[27 + n] for n in range(27)]
    biases = [floats[54], floats[55]]
    camera, first = place[0], place[1]
    spread_filters(k_one, k_two, one, two)
    for load in loads:
        load.wait()
    w_first, w_second = first_w, second_w
    spread_first(w_first, wide)
    last, next_ = wrapped(camera - 2), wrapped(camera + 2)
    third = wrapped(jnp.where((camera & 1) == 0, camera - 3, camera + 3))
    others = [next_, next_ ^ 1, third, last, last ^ 1]
    neighbour_features(others, pictures[...], wide, w_second, place, ids, count, offsets, right)

    zero = jnp.zeros((8 * ROWS, W), BF16)
    for block in (0, BLOCKS + 1):
        vol[block] = zero
        smooth[block] = zero[: 8 * (BAND + 2)]

    scale = jnp.float32(1.0 / 8 / 6)
    for n in range(2, 6):
        scale = jnp.where(count[0] == n, jnp.float32(1.0 / 8 / n), scale)
    swap = one_hot(iota((D, W), 0) + iota((D, W), 1) == D - 1)
    inside = iota((128, 128), 0) + iota((128, 128), 1) >= 127

    for pair in range(ROWS // 2):
        done = []
        for row in (2 * pair, 2 * pair + 1):
            upper, lower = correlated(left, right, row, upper_sum[row], lower_sum[row])
            upper = jnp.where(inside, upper * scale, 0.0)
            lower = lower * scale
            summed = jnp.concatenate(
                [
                    jnp.concatenate([jnp.zeros((128, 128), F32), upper], axis=1),
                    jnp.concatenate([jnp.where(inside, lower[:, :128], 0.0), lower[:, 128:]], axis=1),
                ],
                axis=0,
            )
            turned = pltpu.roll(summed, 1, axis=1, stride=1, stride_axis=0).astype(BF16)
            flipped = lax.dot_general(
                swap, turned, (((1,), (1,)), ((), ())), preferred_element_type=F32
            )
            done.append(flipped.reshape(BLOCKS, 8, W))
        vol[1 : BLOCKS + 1, 16 * pair : 16 * pair + 16, :] = jnp.concatenate(done, axis=1).astype(BF16)

    bias_one, bias_two = biases[0], biases[1]
    above_ok = jnp.where(first > 0, 1.0, 0.0)
    under_ok = jnp.where(first + BAND < H, 1.0, 0.0)

    for block in range(BLOCKS):
        halves = []
        for half in range(2):
            source = vol[block : block + 3, 32 * half : 32 * half + 64, :].reshape(192, W)
            total = jnp.dot(one[half, 0], source, preferred_element_type=F32)
            total = total + jnp.dot(one[half, 1], source, preferred_element_type=F32)
            halves.append(side_sum([total[40 * e : 40 * e + 40] for e in range(3)]))
        result = jnp.maximum(jnp.concatenate(halves, axis=0) + bias_one, 0.0)
        result = jnp.concatenate(
            [result[:8] * above_ok, result[8:72], result[72:] * under_ok], axis=0
        )
        smooth[block + 1] = result.astype(BF16)

    for block in range(BLOCKS):
        source = smooth[block : block + 3].reshape(240, W)
        total = jnp.dot(two[0], source, preferred_element_type=F32)
        total = total + jnp.dot(two[1], source, preferred_element_type=F32)
        result = side_sum([total[64 * e : 64 * e + 64] for e in range(3)]) + bias_two
        out[0, 8 * block : 8 * block + 8] = result.reshape(8, BAND, W).astype(BF16)


VMEM, SMEM = pl.BlockSpec(memory_space=pltpu.VMEM), pl.BlockSpec(memory_space=pltpu.SMEM)
WIDE = pltpu.VMEM((64 * ROWS, TAPS), BF16)


ANY = pl.BlockSpec(memory_space=pl.ANY)
WEIGHTS = [
    pltpu.SemaphoreType.DMA((2,)),
    pltpu.VMEM((27, 64), BF16),
    pltpu.VMEM((64, 64), BF16),
]


def early_sums(table, w_first, w_second, pair):
    return pl.pallas_call(
        early_kernel,
        out_shape=(
            jax.ShapeDtypeStruct((ROWS // 2, 2 * W, 128), BF16),
            jax.ShapeDtypeStruct((ROWS, 128, 128), F32),
            jax.ShapeDtypeStruct((ROWS, 128, W), F32),
        ),
        in_specs=[SMEM, ANY, ANY, VMEM],
        out_specs=(VMEM, VMEM, VMEM),
        scratch_shapes=[WIDE, pltpu.VMEM((1, 64 * ROWS, W), BF16), *WEIGHTS],
        name="early_sums",
        cost_estimate=pl.CostEstimate(flops=2000000000, bytes_accessed=3500000, transcendentals=0),
        compiler_params=pltpu.CompilerParams(vmem_limit_bytes=16 * 1024 * 1024),
    )(table, w_first, w_second, pair)


def cost_volume(table, floats, w_first, w_second, pictures, sums):
    return pl.pallas_call(
        late_kernel,
        out_shape=jax.ShapeDtypeStruct((1, D, BAND, W), BF16),
        in_specs=[SMEM, SMEM, ANY, ANY] + [VMEM] * 4,
        out_specs=VMEM,
        scratch_shapes=[
            WIDE,
            pltpu.VMEM((2, 2, 120, 192), BF16),
            pltpu.VMEM((2, 192, 240), BF16),
            pltpu.VMEM((5, 64 * ROWS, W), BF16),
            pltpu.VMEM((BLOCKS + 2, 8 * ROWS, W), BF16),
            pltpu.VMEM((BLOCKS + 2, 8 * (BAND + 2), W), BF16),
            *WEIGHTS,
        ],
        name="cost_volume",
        cost_estimate=pl.CostEstimate(flops=5000000000, bytes_accessed=4500000, transcendentals=0),
        compiler_params=pltpu.CompilerParams(vmem_limit_bytes=24 * 1024 * 1024),
    )(table, floats, w_first, w_second, pictures, *sums)


def all_of_it(table, floats, w_first, w_second, pair, before, after, far):
    w_first = w_first.T
    sums = early_sums(table, w_first, w_second, pair)
    pictures = jnp.concatenate([after, far[:1], before], axis=0)
    return cost_volume(table, floats, w_first, w_second, pictures, sums)


def from_camera(value, source_of):
    return lax.ppermute(value, "cam", [(source_of(to) % CAMS, to) for to in range(CAMS)])


def on_device(
    images, neighbor_ids, neighbor_count, offsets, w_first, w_second, kernel_one, kernel_two, biases
):
    pair = jnp.concatenate([images, from_camera(images, lambda to: to ^ 1)], axis=0)
    ends = lax.axis_size("rows") - 1
    over = lax.ppermute(pair, "rows", [(i, i + 1) for i in range(ends)])
    under = lax.ppermute(pair, "rows", [(i + 1, i) for i in range(ends)])
    pair = jnp.concatenate([over[:, :, 4:], pair, under[:, :, :4]], axis=2)
    after = from_camera(pair, lambda to: to + 2)
    before = from_camera(pair, lambda to: to - 2)
    far = from_camera(pair, lambda to: to - 3 if to % 2 == 0 else to + 3)
    place = jnp.stack([lax.axis_index("cam"), lax.axis_index("rows") * BAND]).astype(jnp.int32)
    table = jnp.concatenate([place, neighbor_ids[0], offsets[0], neighbor_count])
    floats = jnp.concatenate([kernel_one, kernel_two, biases])
    return all_of_it(table, floats, w_first, w_second, pair, before, after, far)


def solution(mesh):
    in_specs = (
        P("cam", None, "rows", None),
        P("cam", None),
        P("cam"),
        P("cam", None),
        P(),
        P(),
        P(),
        P(),
        P(),
    )
    out_specs = P("cam", None, "rows", None)
    return jax.shard_map(
        on_device, mesh=mesh, in_specs=in_specs, out_specs=out_specs, check_vma=False
    )
```

```python
import jax
import jax.numpy as jnp
from jax import lax
from jax.experimental import pallas as pl
from jax.experimental.pallas import tpu as pltpu
from jax.sharding import PartitionSpec as P

C = 64
D = 192
W = 256
NBR = 6
CAMS = 64
H = 32
BAND = 8
ROWS = BAND + 4
TALL = BAND + 8
TAPS = 9 * TALL
BLOCKS = D // 8
F32 = jnp.float32
BF16 = jnp.bfloat16


def iota(shape, axis):
    return lax.broadcasted_iota(jnp.int32, shape, axis)


def one_hot(condition):
    return condition.astype(F32).astype(BF16)


def spread_first(w_first, wide):
    shape = (32, 256)
    tap, k = iota(shape, 0), iota(shape, 1)
    q = k >> 4
    p = (q * 11) >> 5
    for y in range(ROWS):
        a = (k & 15) - y - 1
        chosen = (a >= 0) & (a <= 2) & (q < 9) & (tap == 6 * p + q + 3 * a)
        taps = lax.dot_general(
            w_first, one_hot(chosen), (((0,), (0,)), ((), ())), preferred_element_type=F32
        )
        wide[64 * y : 64 * y + 64, :] = taps[:, :TAPS].astype(BF16)


def fill_taps(a, b, taps_ref, store):
    masks = [[(a == i) & (b == j) for j in range(3)] for i in range(3)]
    for e in range(3):
        filled = jnp.zeros(a.shape, F32)
        for i in range(3):
            for j in range(3):
                filled = jnp.where(masks[i][j], taps_ref[9 * i + 3 * j + e], filled)
        high = filled.astype(BF16)
        store(e, high, (filled - high.astype(F32)).astype(BF16))


def spread_filters(k_one, k_two, one, two):
    shape = (40, 192)
    m, k = iota(shape, 0), iota(shape, 1)
    a = 8 * (k >> 6) - 7 + (k & 7) - (m & 7)
    b = ((k >> 3) & 7) - (m >> 3)
    for half in range(2):
        parts = [[], []]

        def keep(e, high, low):
            parts[0].append(high.astype(F32))
            parts[1].append(low.astype(F32))

        fill_taps(a, b - half, k_one, keep)
        for n in range(2):
            one[half, n] = jnp.concatenate(parts[n], axis=0).astype(BF16)
    shape = (64, 240)
    m, k = iota(shape, 0), iota(shape, 1)
    q = k >> 3
    t = (q >= 10).astype(jnp.int32) + (q >= 20).astype(jnp.int32)
    a = 8 * t - 7 + (k & 7) - (m >> 3)
    b = (q - 10 * t) - (m & 7)

    def save(e, high, low):
        two[0, 64 * e : 64 * e + 64] = high
        two[1, 64 * e : 64 * e + 64] = low

    fill_taps(a, b, k_two, save)


def turned_columns(value):
    mirror = one_hot(iota((W, W), 0) + iota((W, W), 1) == W - 1)
    return jnp.dot(value, mirror, preferred_element_type=F32)


def columns_of(picture_of, shift):
    lane = iota((TALL, W), 1)
    parts = []
    for p in range(3):
        rows = picture_of(p).astype(F32)
        if shift is not None:
            rows = pltpu.roll(rows, jnp.where(shift > 0, TALL - shift, -shift), axis=0)
        sides = [
            jnp.where(lane == 0, 0.0, pltpu.roll(rows, 1, axis=1)),
            rows,
            jnp.where(lane == W - 1, 0.0, pltpu.roll(rows, W - 1, axis=1)),
        ]
        parts += sides if shift is None else sides[::-1]
    return jnp.concatenate(parts, axis=0).astype(BF16)


def side_sum(parts):
    lane = iota(parts[0].shape, 1)
    left = jnp.where(lane == 0, 0.0, pltpu.roll(parts[0], 1, axis=1))
    right = jnp.where(lane == W - 1, 0.0, pltpu.roll(parts[2], W - 1, axis=1))
    return left + parts[1] + right


def features(columns, wide, w_second, group, top, listed):
    hidden = jnp.dot(wide[256 * group : 256 * group + 256, :], columns, preferred_element_type=F32)
    found = []
    for q in range(4):
        row = top + 4 * group + q
        keep = jnp.where((row >= 0) & (row < H) & listed, 1.0, 0.0)
        part = jnp.maximum(hidden[64 * q : 64 * q + 64], 0.0) * keep
        found.append(jnp.dot(w_second, part.astype(BF16), preferred_element_type=F32))
    return found


def read_table(table):
    value = [table[n] for n in range(15)]
    return value[0:2], value[2:8], value[14:15], value[8:14]


def wrapped(camera):
    return (camera + CAMS) & (CAMS - 1)


def neighbour_features(others, pictures, wide, w_second, place, ids, count, offsets, right):
    number = len(others)
    mirrored = turned_columns(pictures.reshape(number * 3 * TALL, W))
    for index, other in enumerate(others):
        shift, listed = jnp.int32(0), jnp.bool_(False)
        for slot in range(NBR):
            here = (ids[slot] == other) & (slot < count[0])
            shift = jnp.where(here, offsets[slot], shift)
            listed = listed | here
        columns = columns_of(
            lambda p: mirrored[(3 * index + p) * TALL : (3 * index + p + 1) * TALL], shift
        )
        for group in range(3):
            parts = features(columns, wide, w_second, group, place[1] - 2 + shift, listed)
            for q, part in enumerate(parts):
                at = 256 * group + 64 * q
                right[index, at : at + 64] = part.astype(BF16)


def correlated(left, right, row, upper, lower):
    pair, base = row // 2, W * (row % 2)
    top = left[pair, base : base + 128]
    bottom = left[pair, base + 128 : base + 256]
    for index in range(right.shape[0]):
        other = right[index, 128 * pair : 128 * pair + 128, :]
        a = jnp.maximum(jnp.dot(top, other[:, 128:], preferred_element_type=F32), 0.0)
        b = jnp.maximum(jnp.dot(bottom, other, preferred_element_type=F32), 0.0)
        upper = a if upper is None else upper + a
        lower = b if lower is None else lower + b
    return upper, lower


def early_kernel(table, weights, pictures, left, upper, lower, wide, right):
    place, ids, count, offsets = read_table(table)
    columns = columns_of(lambda p: pictures[0, p], None)
    w_second = weights[0:64]
    spread_first(weights[64:96], wide)
    lane = iota((W, 128), 1)
    for group in range(3):
        found = features(columns, wide, w_second, group, place[1] - 2, True)
        for half in range(2):
            pair = jnp.concatenate(found[2 * half : 2 * half + 2], axis=0).T
            left[2 * group + half, 0:W] = jnp.where(lane < 64, pair, 0.0).astype(BF16)
            left[2 * group + half, W : 2 * W] = jnp.where(lane >= 64, pair, 0.0).astype(BF16)
    neighbour_features(
        [place[0] ^ 1], pictures[1], wide, w_second, place, ids, count, offsets, right
    )
    for row in range(ROWS):
        upper[row], lower[row] = correlated(left, right, row, None, None)


def late_kernel(
    table, floats, weights, pictures, left, upper_sum, lower_sum, wide, out, one, two, right, vol, smooth, result, sems
):
    place, ids, count, offsets = read_table(table)
    k_one = [floats[n] for n in range(27)]
    k_two = [floats[27 + n] for n in range(27)]
    biases = [floats[54], floats[55]]
    camera, first = place[0], place[1]
    w_second = weights[0:64]
    spread_filters(k_one, k_two, one, two)
    last, next_ = wrapped(camera - 2), wrapped(camera + 2)
    third = wrapped(jnp.where((camera & 1) == 0, camera - 3, camera + 3))
    others = [next_, next_ ^ 1, third, last, last ^ 1]
    neighbour_features(others, pictures[...], wide, w_second, place, ids, count, offsets, right)

    zero = jnp.zeros((8 * ROWS, W), BF16)
    for block in (0, BLOCKS + 1):
        vol[block] = zero
        smooth[block] = zero[: 8 * (BAND + 2)]

    scale = jnp.float32(1.0 / 8 / 6)
    for n in range(2, 6):
        scale = jnp.where(count[0] == n, jnp.float32(1.0 / 8 / n), scale)
    swap = one_hot(iota((D, W), 0) + iota((D, W), 1) == D - 1)
    inside = iota((128, 128), 0) + iota((128, 128), 1) >= 127

    for pair in range(ROWS // 2):
        done = []
        for row in (2 * pair, 2 * pair + 1):
            upper, lower = correlated(left, right, row, upper_sum[row], lower_sum[row])
            upper = jnp.where(inside, upper * scale, 0.0)
            lower = lower * scale
            summed = jnp.concatenate(
                [
                    jnp.concatenate([jnp.zeros((128, 128), F32), upper], axis=1),
                    jnp.concatenate([jnp.where(inside, lower[:, :128], 0.0), lower[:, 128:]], axis=1),
                ],
                axis=0,
            )
            turned = pltpu.roll(summed, 1, axis=1, stride=1, stride_axis=0).astype(BF16)
            flipped = lax.dot_general(
                swap, turned, (((1,), (1,)), ((), ())), preferred_element_type=F32
            )
            done.append(flipped.reshape(BLOCKS, 8, W))
        vol[1 : BLOCKS + 1, 16 * pair : 16 * pair + 16, :] = jnp.concatenate(done, axis=1).astype(BF16)

    bias_one, bias_two = biases[0], biases[1]
    above_ok = jnp.where(first > 0, 1.0, 0.0)
    under_ok = jnp.where(first + BAND < H, 1.0, 0.0)

    for block in range(BLOCKS):
        halves = []
        for half in range(2):
            source = vol[block : block + 3, 32 * half : 32 * half + 64, :].reshape(192, W)
            total = jnp.dot(one[half, 0], source, preferred_element_type=F32)
            total = total + jnp.dot(one[half, 1], source, preferred_element_type=F32)
            halves.append(side_sum([total[40 * e : 40 * e + 40] for e in range(3)]))
        hidden = jnp.maximum(jnp.concatenate(halves, axis=0) + bias_one, 0.0)
        hidden = jnp.concatenate(
            [hidden[:8] * above_ok, hidden[8:72], hidden[72:] * under_ok], axis=0
        )
        smooth[block + 1] = hidden.astype(BF16)

    stores = []
    for block in range(BLOCKS):
        source = smooth[block : block + 3].reshape(240, W)
        total = jnp.dot(two[0], source, preferred_element_type=F32)
        total = total + jnp.dot(two[1], source, preferred_element_type=F32)
        filtered = side_sum([total[64 * e : 64 * e + 64] for e in range(3)]) + bias_two
        result[8 * block : 8 * block + 8] = filtered.reshape(8, BAND, W).astype(BF16)
        if block % 4 == 3:
            part = pl.ds(8 * block - 24, 32)
            stores.append(pltpu.make_async_copy(result.at[part], out.at[0, part], sems.at[block // 4]))
            stores[-1].start()
    for store in stores:
        store.wait()


VMEM, SMEM = pl.BlockSpec(memory_space=pltpu.VMEM), pl.BlockSpec(memory_space=pltpu.SMEM)


ANY = pl.BlockSpec(memory_space=pl.ANY)
def early_sums(table, weights, pair):
    return pl.pallas_call(
        early_kernel,
        out_shape=(
            jax.ShapeDtypeStruct((ROWS // 2, 2 * W, 128), BF16),
            jax.ShapeDtypeStruct((ROWS, 128, 128), F32),
            jax.ShapeDtypeStruct((ROWS, 128, W), F32),
            jax.ShapeDtypeStruct((64 * ROWS, TAPS), BF16),
        ),
        in_specs=[SMEM, VMEM, VMEM],
        out_specs=(VMEM,) * 4,
        scratch_shapes=[pltpu.VMEM((1, 64 * ROWS, W), BF16)],
        name="early_sums",
        cost_estimate=pl.CostEstimate(flops=2000000000, bytes_accessed=3500000, transcendentals=0),
        compiler_params=pltpu.CompilerParams(vmem_limit_bytes=16 * 1024 * 1024),
    )(table, weights, pair)


def cost_volume(table, floats, weights, pictures, sums):
    return pl.pallas_call(
        late_kernel,
        out_shape=jax.ShapeDtypeStruct((1, D, BAND, W), BF16),
        in_specs=[SMEM] * 2 + [VMEM] * 6,
        out_specs=ANY,
        scratch_shapes=[
            pltpu.VMEM((2, 2, 120, 192), BF16),
            pltpu.VMEM((2, 192, 240), BF16),
            pltpu.VMEM((5, 64 * ROWS, W), BF16),
            pltpu.VMEM((BLOCKS + 2, 8 * ROWS, W), BF16),
            pltpu.VMEM((BLOCKS + 2, 8 * (BAND + 2), W), BF16),
            pltpu.VMEM((D, BAND, W), BF16),
            pltpu.SemaphoreType.DMA((BLOCKS // 4,)),
        ],
        name="cost_volume",
        cost_estimate=pl.CostEstimate(flops=5000000000, bytes_accessed=4500000, transcendentals=0),
        compiler_params=pltpu.CompilerParams(vmem_limit_bytes=24 * 1024 * 1024),
    )(table, floats, weights, pictures, *sums)


def all_of_it(table, floats, weights, pair, before, after, far):
    sums = early_sums(table, weights, pair)
    pictures = jnp.concatenate([after, far[:1], before], axis=0)
    return cost_volume(table, floats, weights, pictures, sums)


def from_camera(value, source_of):
    return lax.ppermute(value, "cam", [(source_of(to) % CAMS, to) for to in range(CAMS)])


def on_device(
    images, neighbor_ids, neighbor_count, offsets, w_first, w_second, kernel_one, kernel_two, biases
):
    pair = jnp.concatenate([images, from_camera(images, lambda to: to ^ 1)], axis=0)
    ends = lax.axis_size("rows") - 1
    over = lax.ppermute(pair, "rows", [(i, i + 1) for i in range(ends)])
    under = lax.ppermute(pair, "rows", [(i + 1, i) for i in range(ends)])
    pair = jnp.concatenate([over[:, :, 4:], pair, under[:, :, :4]], axis=2)
    after = from_camera(pair, lambda to: to + 2)
    before = from_camera(pair, lambda to: to - 2)
    far = from_camera(pair, lambda to: to - 3 if to % 2 == 0 else to + 3)
    place = jnp.stack([lax.axis_index("cam"), lax.axis_index("rows") * BAND]).astype(jnp.int32)
    table = jnp.concatenate([place, neighbor_ids[0], offsets[0], neighbor_count])
    floats = jnp.concatenate([kernel_one, kernel_two, biases])
    weights = jnp.concatenate([w_second, jnp.pad(w_first.T, ((0, 5), (0, 0)))], axis=0)
    return all_of_it(table, floats, weights, pair, before, after, far)


def solution(mesh):
    in_specs = (
        P("cam", None, "rows", None),
        P("cam", None),
        P("cam"),
        P("cam", None),
        P(),
        P(),
        P(),
        P(),
        P(),
    )
    out_specs = P("cam", None, "rows", None)
    return jax.shard_map(
        on_device, mesh=mesh, in_specs=in_specs, out_specs=out_specs, check_vma=False
    )
```

```python
import jax
import jax.numpy as jnp
from jax import lax
from jax.experimental import pallas as pl
from jax.experimental.pallas import tpu as pltpu
from jax.sharding import PartitionSpec as P

C = 64
D = 192
W = 256
NBR = 6
CAMS = 64
H = 32
BAND = 8
ROWS = BAND + 4
TALL = BAND + 8
TAPS = 9 * TALL
BLOCKS = D // 8
F32 = jnp.float32
BF16 = jnp.bfloat16


def iota(shape, axis):
    return lax.broadcasted_iota(jnp.int32, shape, axis)


def one_hot(condition):
    return condition.astype(F32).astype(BF16)


def spread_first(w_first, wide):
    shape = (32, 256)
    tap, k = iota(shape, 0), iota(shape, 1)
    q = k >> 4
    p = (q * 11) >> 5
    for y in range(ROWS):
        a = (k & 15) - y - 1
        chosen = (a >= 0) & (a <= 2) & (q < 9) & (tap == 6 * p + q + 3 * a)
        taps = lax.dot_general(
            w_first, one_hot(chosen), (((0,), (0,)), ((), ())), preferred_element_type=F32
        )
        wide[64 * y : 64 * y + 64, :] = taps[:, :TAPS].astype(BF16)


def fill_taps(a, b, taps_ref, store):
    masks = [[(a == i) & (b == j) for j in range(3)] for i in range(3)]
    for e in range(3):
        filled = jnp.zeros(a.shape, F32)
        for i in range(3):
            for j in range(3):
                filled = jnp.where(masks[i][j], taps_ref[9 * i + 3 * j + e], filled)
        high = filled.astype(BF16)
        store(e, high, (filled - high.astype(F32)).astype(BF16))


def spread_filters(k_one, k_two, one, two):
    shape = (40, 192)
    m, k = iota(shape, 0), iota(shape, 1)
    a = 8 * (k >> 6) - 7 + (k & 7) - (m & 7)
    b = ((k >> 3) & 7) - (m >> 3)
    for half in range(2):
        parts = [[], []]

        def keep(e, high, low):
            parts[0].append(high.astype(F32))
            parts[1].append(low.astype(F32))

        fill_taps(a, b - half, k_one, keep)
        for n in range(2):
            one[half, n] = jnp.concatenate(parts[n], axis=0).astype(BF16)
    shape = (64, 240)
    m, k = iota(shape, 0), iota(shape, 1)
    q = k >> 3
    t = (q >= 10).astype(jnp.int32) + (q >= 20).astype(jnp.int32)
    a = 8 * t - 7 + (k & 7) - (m >> 3)
    b = (q - 10 * t) - (m & 7)

    def save(e, high, low):
        two[0, 64 * e : 64 * e + 64] = high
        two[1, 64 * e : 64 * e + 64] = low

    fill_taps(a, b, k_two, save)


def turned_columns(value):
    mirror = one_hot(iota((W, W), 0) + iota((W, W), 1) == W - 1)
    return jnp.dot(value, mirror, preferred_element_type=F32)


def columns_of(picture_of, shift):
    lane = iota((TALL, W), 1)
    parts = []
    for p in range(3):
        rows = picture_of(p).astype(F32)
        if shift is not None:
            rows = pltpu.roll(rows, jnp.where(shift > 0, TALL - shift, -shift), axis=0)
        sides = [
            jnp.where(lane == 0, 0.0, pltpu.roll(rows, 1, axis=1)),
            rows,
            jnp.where(lane == W - 1, 0.0, pltpu.roll(rows, W - 1, axis=1)),
        ]
        parts += sides if shift is None else sides[::-1]
    return jnp.concatenate(parts, axis=0).astype(BF16)


def side_sum(parts):
    lane = iota(parts[0].shape, 1)
    left = jnp.where(lane == 0, 0.0, pltpu.roll(parts[0], 1, axis=1))
    right = jnp.where(lane == W - 1, 0.0, pltpu.roll(parts[2], W - 1, axis=1))
    return left + parts[1] + right


def features(columns, wide, w_second, group, top, listed):
    hidden = jnp.dot(wide[256 * group : 256 * group + 256, :], columns, preferred_element_type=F32)
    found = []
    for q in range(4):
        row = top + 4 * group + q
        keep = jnp.where((row >= 0) & (row < H) & listed, 1.0, 0.0)
        part = jnp.maximum(hidden[64 * q : 64 * q + 64], 0.0) * keep
        found.append(jnp.dot(w_second, part.astype(BF16), preferred_element_type=F32))
    return found


def read_table(table):
    value = [table[n] for n in range(15)]
    return value[0:2], value[2:8], value[14:15], value[8:14]


def wrapped(camera):
    return (camera + CAMS) & (CAMS - 1)


def neighbour_features(others, pictures, wide, w_second, place, ids, count, offsets, right):
    number = len(others)
    mirrored = turned_columns(pictures.reshape(number * 3 * TALL, W))
    for index, other in enumerate(others):
        shift, listed = jnp.int32(0), jnp.bool_(False)
        for slot in range(NBR):
            here = (ids[slot] == other) & (slot < count[0])
            shift = jnp.where(here, offsets[slot], shift)
            listed = listed | here
        columns = columns_of(
            lambda p: mirrored[(3 * index + p) * TALL : (3 * index + p + 1) * TALL], shift
        )
        for group in range(3):
            parts = features(columns, wide, w_second, group, place[1] - 2 + shift, listed)
            for q, part in enumerate(parts):
                at = 256 * group + 64 * q
                right[index, at : at + 64] = part.astype(BF16)


def correlated(left, right, pair, upper, lower):
    for index in range(right.shape[0]):
        other = right[index, 128 * pair : 128 * pair + 128, :]
        a = jnp.maximum(jnp.dot(left[pair, 0:256], other[:, 128:], preferred_element_type=F32), 0.0)
        b = jnp.maximum(jnp.dot(left[pair, 256:512], other, preferred_element_type=F32), 0.0)
        upper = a if upper is None else upper + a
        lower = b if lower is None else lower + b
    return upper, lower


def early_kernel(table, weights, pictures, left, upper, lower, wide, right):
    place, ids, count, offsets = read_table(table)
    columns = columns_of(lambda p: pictures[0, p], None)
    w_second = weights[0:64]
    spread_first(weights[64:96], wide)
    lane = iota((W, 128), 1)
    for group in range(3):
        found = features(columns, wide, w_second, group, place[1] - 2, True)
        for half in range(2):
            pair = jnp.concatenate(found[2 * half : 2 * half + 2], axis=0).T
            one_row = jnp.where(lane < 64, pair, 0.0).astype(BF16)
            next_row = jnp.where(lane >= 64, pair, 0.0).astype(BF16)
            at = 2 * group + half
            left[at, 0:128], left[at, 128:256] = one_row[:128], next_row[:128]
            left[at, 256:384], left[at, 384:512] = one_row[128:], next_row[128:]
    neighbour_features(
        [place[0] ^ 1], pictures[1], wide, w_second, place, ids, count, offsets, right
    )
    for pair in range(ROWS // 2):
        upper[pair], lower[pair] = correlated(left, right, pair, None, None)


def late_kernel(
    table, floats, weights, pictures, left, upper_sum, lower_sum, wide, out, one, two, right, vol, smooth, result, sems
):
    place, ids, count, offsets = read_table(table)
    k_one = [floats[n] for n in range(27)]
    k_two = [floats[27 + n] for n in range(27)]
    biases = [floats[54], floats[55]]
    camera, first = place[0], place[1]
    w_second = weights[0:64]
    spread_filters(k_one, k_two, one, two)
    last, next_ = wrapped(camera - 2), wrapped(camera + 2)
    third = wrapped(jnp.where((camera & 1) == 0, camera - 3, camera + 3))
    others = [next_, next_ ^ 1, third, last, last ^ 1]
    neighbour_features(others, pictures[...], wide, w_second, place, ids, count, offsets, right)

    zero = jnp.zeros((8 * ROWS, W), BF16)
    for block in (0, BLOCKS + 1):
        vol[block] = zero
        smooth[block] = zero[: 8 * (BAND + 2)]

    scale = jnp.float32(1.0 / 8 / 6)
    for n in range(2, 6):
        scale = jnp.where(count[0] == n, jnp.float32(1.0 / 8 / n), scale)
    swap = one_hot(iota((D, W), 0) + iota((D, W), 1) == D - 1)
    inside = iota((128, 128), 0) + iota((128, 128), 1) >= 127

    for pair in range(ROWS // 2):
        done = []
        uppers, lowers = correlated(left, right, pair, upper_sum[pair], lower_sum[pair])
        for row in range(2):
            upper, lower = uppers[128 * row : 128 * row + 128], lowers[128 * row : 128 * row + 128]
            upper = jnp.where(inside, upper * scale, 0.0)
            lower = lower * scale
            summed = jnp.concatenate(
                [
                    jnp.concatenate([jnp.zeros((128, 128), F32), upper], axis=1),
                    jnp.concatenate([jnp.where(inside, lower[:, :128], 0.0), lower[:, 128:]], axis=1),
                ],
                axis=0,
            )
            turned = pltpu.roll(summed, 1, axis=1, stride=1, stride_axis=0).astype(BF16)
            flipped = lax.dot_general(
                swap, turned, (((1,), (1,)), ((), ())), preferred_element_type=F32
            )
            done.append(flipped.reshape(BLOCKS, 8, W))
        vol[1 : BLOCKS + 1, 16 * pair : 16 * pair + 16, :] = jnp.concatenate(done, axis=1).astype(BF16)

    bias_one, bias_two = biases[0], biases[1]
    above_ok = jnp.where(first > 0, 1.0, 0.0)
    under_ok = jnp.where(first + BAND < H, 1.0, 0.0)

    for block in range(BLOCKS):
        halves = []
        for half in range(2):
            source = vol[block : block + 3, 32 * half : 32 * half + 64, :].reshape(192, W)
            total = jnp.dot(one[half, 0], source, preferred_element_type=F32)
            total = total + jnp.dot(one[half, 1], source, preferred_element_type=F32)
            halves.append(side_sum([total[40 * e : 40 * e + 40] for e in range(3)]))
        hidden = jnp.maximum(jnp.concatenate(halves, axis=0) + bias_one, 0.0)
        hidden = jnp.concatenate(
            [hidden[:8] * above_ok, hidden[8:72], hidden[72:] * under_ok], axis=0
        )
        smooth[block + 1] = hidden.astype(BF16)

    stores = []
    for block in range(BLOCKS):
        source = smooth[block : block + 3].reshape(240, W)
        total = jnp.dot(two[0], source, preferred_element_type=F32)
        total = total + jnp.dot(two[1], source, preferred_element_type=F32)
        filtered = side_sum([total[64 * e : 64 * e + 64] for e in range(3)]) + bias_two
        result[8 * block : 8 * block + 8] = filtered.reshape(8, BAND, W).astype(BF16)
        if block % 4 == 3:
            part = pl.ds(8 * block - 24, 32)
            stores.append(pltpu.make_async_copy(result.at[part], out.at[0, part], sems.at[block // 4]))
            stores[-1].start()
    for store in stores:
        store.wait()


VMEM, SMEM = pl.BlockSpec(memory_space=pltpu.VMEM), pl.BlockSpec(memory_space=pltpu.SMEM)


ANY = pl.BlockSpec(memory_space=pl.ANY)
def early_sums(table, weights, pair):
    return pl.pallas_call(
        early_kernel,
        out_shape=(
            jax.ShapeDtypeStruct((ROWS // 2, 2 * W, 128), BF16),
            jax.ShapeDtypeStruct((ROWS // 2, 256, 128), F32),
            jax.ShapeDtypeStruct((ROWS // 2, 256, W), F32),
            jax.ShapeDtypeStruct((64 * ROWS, TAPS), BF16),
        ),
        in_specs=[SMEM, VMEM, VMEM],
        out_specs=(VMEM,) * 4,
        scratch_shapes=[pltpu.VMEM((1, 64 * ROWS, W), BF16)],
        name="early_sums",
        cost_estimate=pl.CostEstimate(flops=2000000000, bytes_accessed=3500000, transcendentals=0),
        compiler_params=pltpu.CompilerParams(vmem_limit_bytes=16 * 1024 * 1024),
    )(table, weights, pair)


def cost_volume(table, floats, weights, pictures, sums):
    return pl.pallas_call(
        late_kernel,
        out_shape=jax.ShapeDtypeStruct((1, D, BAND, W), BF16),
        in_specs=[SMEM] * 2 + [VMEM] * 6,
        out_specs=ANY,
        scratch_shapes=[
            pltpu.VMEM((2, 2, 120, 192), BF16),
            pltpu.VMEM((2, 192, 240), BF16),
            pltpu.VMEM((5, 64 * ROWS, W), BF16),
            pltpu.VMEM((BLOCKS + 2, 8 * ROWS, W), BF16),
            pltpu.VMEM((BLOCKS + 2, 8 * (BAND + 2), W), BF16),
            pltpu.VMEM((D, BAND, W), BF16),
            pltpu.SemaphoreType.DMA((BLOCKS // 4,)),
        ],
        name="cost_volume",
        cost_estimate=pl.CostEstimate(flops=5000000000, bytes_accessed=4500000, transcendentals=0),
        compiler_params=pltpu.CompilerParams(vmem_limit_bytes=24 * 1024 * 1024),
    )(table, floats, weights, pictures, *sums)


def all_of_it(table, floats, weights, pair, before, after, far):
    sums = early_sums(table, weights, pair)
    pictures = jnp.concatenate([after, far[:1], before], axis=0)
    return cost_volume(table, floats, weights, pictures, sums)


def from_camera(value, source_of):
    return lax.ppermute(value, "cam", [(source_of(to) % CAMS, to) for to in range(CAMS)])


def on_device(
    images, neighbor_ids, neighbor_count, offsets, w_first, w_second, kernel_one, kernel_two, biases
):
    pair = jnp.concatenate([images, from_camera(images, lambda to: to ^ 1)], axis=0)
    ends = lax.axis_size("rows") - 1
    over = lax.ppermute(pair, "rows", [(i, i + 1) for i in range(ends)])
    under = lax.ppermute(pair, "rows", [(i + 1, i) for i in range(ends)])
    pair = jnp.concatenate([over[:, :, 4:], pair, under[:, :, :4]], axis=2)
    after = from_camera(pair, lambda to: to + 2)
    before = from_camera(pair, lambda to: to - 2)
    far = from_camera(pair, lambda to: to - 3 if to % 2 == 0 else to + 3)
    place = jnp.stack([lax.axis_index("cam"), lax.axis_index("rows") * BAND]).astype(jnp.int32)
    table = jnp.concatenate([place, neighbor_ids[0], offsets[0], neighbor_count])
    floats = jnp.concatenate([kernel_one, kernel_two, biases])
    weights = jnp.concatenate([w_second, jnp.pad(w_first.T, ((0, 5), (0, 0)))], axis=0)
    return all_of_it(table, floats, weights, pair, before, after, far)


def solution(mesh):
    in_specs = (
        P("cam", None, "rows", None),
        P("cam", None),
        P("cam"),
        P("cam", None),
        P(),
        P(),
        P(),
        P(),
        P(),
    )
    out_specs = P("cam", None, "rows", None)
    return jax.shard_map(
        on_device, mesh=mesh, in_specs=in_specs, out_specs=out_specs, check_vma=False
    )
```

```python
import jax
import jax.numpy as jnp
from jax import lax
from jax.experimental import pallas as pl
from jax.experimental.pallas import tpu as pltpu
from jax.sharding import PartitionSpec as P

C = 64
D = 192
W = 256
NBR = 6
CAMS = 64
H = 32
BAND = 8
ROWS = BAND + 4
TALL = BAND + 8
TAPS = 9 * TALL
BLOCKS = D // 8
F32 = jnp.float32
BF16 = jnp.bfloat16


def iota(shape, axis):
    return lax.broadcasted_iota(jnp.int32, shape, axis)


def one_hot(condition):
    return condition.astype(F32).astype(BF16)


def spread_first(w_first, wide):
    shape = (32, 256)
    tap, k = iota(shape, 0), iota(shape, 1)
    q = k >> 4
    p = (q * 11) >> 5
    for y in range(ROWS):
        a = (k & 15) - y - 1
        chosen = (a >= 0) & (a <= 2) & (q < 9) & (tap == 6 * p + q + 3 * a)
        taps = lax.dot_general(
            w_first, one_hot(chosen), (((0,), (0,)), ((), ())), preferred_element_type=F32
        )
        wide[64 * y : 64 * y + 64, :] = taps[:, :TAPS].astype(BF16)


def fill_taps(a, b, taps_ref, store):
    masks = [[(a == i) & (b == j) for j in range(3)] for i in range(3)]
    for e in range(3):
        filled = jnp.zeros(a.shape, F32)
        for i in range(3):
            for j in range(3):
                filled = jnp.where(masks[i][j], taps_ref[9 * i + 3 * j + e], filled)
        high = filled.astype(BF16)
        store(e, high, (filled - high.astype(F32)).astype(BF16))


def spread_filters(k_one, k_two, one, two):
    shape = (40, 192)
    m, k = iota(shape, 0), iota(shape, 1)
    a = 8 * (k >> 6) - 7 + (k & 7) - (m & 7)
    b = ((k >> 3) & 7) - (m >> 3)
    for half in range(2):
        parts = [[], []]

        def keep(e, high, low):
            parts[0].append(high.astype(F32))
            parts[1].append(low.astype(F32))

        fill_taps(a, b - half, k_one, keep)
        for n in range(2):
            one[half, n] = jnp.concatenate(parts[n], axis=0).astype(BF16)
    shape = (64, 240)
    m, k = iota(shape, 0), iota(shape, 1)
    q = k >> 3
    t = (q >= 10).astype(jnp.int32) + (q >= 20).astype(jnp.int32)
    a = 8 * t - 7 + (k & 7) - (m >> 3)
    b = (q - 10 * t) - (m & 7)

    def save(e, high, low):
        two[0, 64 * e : 64 * e + 64] = high
        two[1, 64 * e : 64 * e + 64] = low

    fill_taps(a, b, k_two, save)


def turned_columns(value):
    mirror = one_hot(iota((W, W), 0) + iota((W, W), 1) == W - 1)
    return jnp.dot(value, mirror, preferred_element_type=F32)


def columns_of(picture_of, shift):
    lane = iota((TALL, W), 1)
    parts = []
    for p in range(3):
        rows = picture_of(p).astype(F32)
        if shift is not None:
            rows = pltpu.roll(rows, jnp.where(shift > 0, TALL - shift, -shift), axis=0)
        sides = [
            jnp.where(lane == 0, 0.0, pltpu.roll(rows, 1, axis=1)),
            rows,
            jnp.where(lane == W - 1, 0.0, pltpu.roll(rows, W - 1, axis=1)),
        ]
        parts += sides if shift is None else sides[::-1]
    return jnp.concatenate(parts, axis=0).astype(BF16)


def side_sum(parts):
    lane = iota(parts[0].shape, 1)
    left = jnp.where(lane == 0, 0.0, pltpu.roll(parts[0], 1, axis=1))
    right = jnp.where(lane == W - 1, 0.0, pltpu.roll(parts[2], W - 1, axis=1))
    return left + parts[1] + right


def features(columns, wide, w_second, group, top, listed):
    hidden = jnp.dot(wide[256 * group : 256 * group + 256, :], columns, preferred_element_type=F32)
    found = []
    for q in range(4):
        row = top + 4 * group + q
        keep = jnp.where((row >= 0) & (row < H) & listed, 1.0, 0.0)
        part = jnp.maximum(hidden[64 * q : 64 * q + 64], 0.0) * keep
        found.append(jnp.dot(w_second, part.astype(BF16), preferred_element_type=F32))
    return found


def read_table(table):
    value = [table[n] for n in range(15)]
    return value[0:2], value[2:8], value[14:15], value[8:14]


def wrapped(camera):
    return (camera + CAMS) & (CAMS - 1)


def neighbour_features(others, pictures, wide, w_second, place, ids, count, offsets, right):
    number = len(others)
    mirrored = turned_columns(pictures.reshape(number * 3 * TALL, W))
    for index, other in enumerate(others):
        shift, listed = jnp.int32(0), jnp.bool_(False)
        for slot in range(NBR):
            here = (ids[slot] == other) & (slot < count[0])
            shift = jnp.where(here, offsets[slot], shift)
            listed = listed | here
        columns = columns_of(
            lambda p: mirrored[(3 * index + p) * TALL : (3 * index + p + 1) * TALL], shift
        )
        for group in range(3):
            parts = features(columns, wide, w_second, group, place[1] - 2 + shift, listed)
            for q, part in enumerate(parts):
                at = 256 * group + 64 * q
                right[index, at : at + 64] = part.astype(BF16)


def correlated(left, right, pair, upper, lower):
    for index in range(right.shape[0]):
        other = right[index, 128 * pair : 128 * pair + 128, :]
        a = jnp.maximum(jnp.dot(left[pair, 0:256], other[:, 128:], preferred_element_type=F32), 0.0)
        b = jnp.maximum(jnp.dot(left[pair, 256:512], other, preferred_element_type=F32), 0.0)
        upper = a if upper is None else upper + a
        lower = b if lower is None else lower + b
    return upper, lower


def early_kernel(table, floats, weights, pictures, left, upper, lower, wide, one, two, right):
    k_one = [floats[n] for n in range(27)]
    k_two = [floats[27 + n] for n in range(27)]
    spread_filters(k_one, k_two, one, two)
    place, ids, count, offsets = read_table(table)
    columns = columns_of(lambda p: pictures[0, p], None)
    w_second = weights[0:64]
    spread_first(weights[64:96], wide)
    lane = iota((W, 128), 1)
    for group in range(3):
        found = features(columns, wide, w_second, group, place[1] - 2, True)
        for half in range(2):
            pair = jnp.concatenate(found[2 * half : 2 * half + 2], axis=0).T
            one_row = jnp.where(lane < 64, pair, 0.0).astype(BF16)
            next_row = jnp.where(lane >= 64, pair, 0.0).astype(BF16)
            at = 2 * group + half
            left[at, 0:128], left[at, 128:256] = one_row[:128], next_row[:128]
            left[at, 256:384], left[at, 384:512] = one_row[128:], next_row[128:]
    neighbour_features(
        [place[0] ^ 1], pictures[1], wide, w_second, place, ids, count, offsets, right
    )
    for pair in range(ROWS // 2):
        upper[pair], lower[pair] = correlated(left, right, pair, None, None)


def late_kernel(
    table, floats, weights, pictures, left, upper_sum, lower_sum, wide, one, two, out, right, vol, smooth, result, sems
):
    place, ids, count, offsets = read_table(table)
    biases = [floats[54], floats[55]]
    camera, first = place[0], place[1]
    w_second = weights[0:64]
    last, next_ = wrapped(camera - 2), wrapped(camera + 2)
    third = wrapped(jnp.where((camera & 1) == 0, camera - 3, camera + 3))
    others = [next_, next_ ^ 1, third, last, last ^ 1]
    neighbour_features(others, pictures[...], wide, w_second, place, ids, count, offsets, right)

    zero = jnp.zeros((8 * ROWS, W), BF16)
    for block in (0, BLOCKS + 1):
        vol[block] = zero
        smooth[block] = zero[: 8 * (BAND + 2)]

    scale = jnp.float32(1.0 / 8 / 6)
    for n in range(2, 6):
        scale = jnp.where(count[0] == n, jnp.float32(1.0 / 8 / n), scale)
    swap = one_hot(iota((D, W), 0) + iota((D, W), 1) == D - 1)
    inside = iota((128, 128), 0) + iota((128, 128), 1) >= 127

    for pair in range(ROWS // 2):
        done = []
        uppers, lowers = correlated(left, right, pair, upper_sum[pair], lower_sum[pair])
        for row in range(2):
            upper, lower = uppers[128 * row : 128 * row + 128], lowers[128 * row : 128 * row + 128]
            upper = jnp.where(inside, upper * scale, 0.0)
            lower = lower * scale
            summed = jnp.concatenate(
                [
                    jnp.concatenate([jnp.zeros((128, 128), F32), upper], axis=1),
                    jnp.concatenate([jnp.where(inside, lower[:, :128], 0.0), lower[:, 128:]], axis=1),
                ],
                axis=0,
            )
            turned = pltpu.roll(summed, 1, axis=1, stride=1, stride_axis=0).astype(BF16)
            flipped = lax.dot_general(
                swap, turned, (((1,), (1,)), ((), ())), preferred_element_type=F32
            )
            done.append(flipped.reshape(BLOCKS, 8, W))
        vol[1 : BLOCKS + 1, 16 * pair : 16 * pair + 16, :] = jnp.concatenate(done, axis=1).astype(BF16)

    bias_one, bias_two = biases[0], biases[1]
    above_ok = jnp.where(first > 0, 1.0, 0.0)
    under_ok = jnp.where(first + BAND < H, 1.0, 0.0)

    for block in range(BLOCKS):
        halves = []
        for half in range(2):
            source = vol[block : block + 3, 32 * half : 32 * half + 64, :].reshape(192, W)
            total = jnp.dot(one[half, 0], source, preferred_element_type=F32)
            total = total + jnp.dot(one[half, 1], source, preferred_element_type=F32)
            halves.append(side_sum([total[40 * e : 40 * e + 40] for e in range(3)]))
        hidden = jnp.maximum(jnp.concatenate(halves, axis=0) + bias_one, 0.0)
        hidden = jnp.concatenate(
            [hidden[:8] * above_ok, hidden[8:72], hidden[72:] * under_ok], axis=0
        )
        smooth[block + 1] = hidden.astype(BF16)

    stores = []
    for block in range(BLOCKS):
        source = smooth[block : block + 3].reshape(240, W)
        total = jnp.dot(two[0], source, preferred_element_type=F32)
        total = total + jnp.dot(two[1], source, preferred_element_type=F32)
        filtered = side_sum([total[64 * e : 64 * e + 64] for e in range(3)]) + bias_two
        result[8 * block : 8 * block + 8] = filtered.reshape(8, BAND, W).astype(BF16)
        if block % 4 == 3:
            part = pl.ds(8 * block - 24, 32)
            stores.append(pltpu.make_async_copy(result.at[part], out.at[0, part], sems.at[block // 4]))
            stores[-1].start()
    for store in stores:
        store.wait()


VMEM, SMEM = pl.BlockSpec(memory_space=pltpu.VMEM), pl.BlockSpec(memory_space=pltpu.SMEM)


ANY = pl.BlockSpec(memory_space=pl.ANY)
def early_sums(table, floats, weights, pair):
    return pl.pallas_call(
        early_kernel,
        out_shape=(
            jax.ShapeDtypeStruct((ROWS // 2, 2 * W, 128), BF16),
            jax.ShapeDtypeStruct((ROWS // 2, 256, 128), F32),
            jax.ShapeDtypeStruct((ROWS // 2, 256, W), F32),
            jax.ShapeDtypeStruct((64 * ROWS, TAPS), BF16),
            jax.ShapeDtypeStruct((2, 2, 120, 192), BF16),
            jax.ShapeDtypeStruct((2, 192, 240), BF16),
        ),
        in_specs=[SMEM, SMEM, VMEM, VMEM],
        out_specs=(VMEM,) * 6,
        scratch_shapes=[pltpu.VMEM((1, 64 * ROWS, W), BF16)],
        name="early_sums",
        cost_estimate=pl.CostEstimate(flops=2000000000, bytes_accessed=3500000, transcendentals=0),
        compiler_params=pltpu.CompilerParams(vmem_limit_bytes=16 * 1024 * 1024),
    )(table, floats, weights, pair)


def cost_volume(table, floats, weights, pictures, sums):
    return pl.pallas_call(
        late_kernel,
        out_shape=jax.ShapeDtypeStruct((1, D, BAND, W), BF16),
        in_specs=[SMEM] * 2 + [VMEM] * 8,
        out_specs=ANY,
        scratch_shapes=[
            pltpu.VMEM((5, 64 * ROWS, W), BF16),
            pltpu.VMEM((BLOCKS + 2, 8 * ROWS, W), BF16),
            pltpu.VMEM((BLOCKS + 2, 8 * (BAND + 2), W), BF16),
            pltpu.VMEM((D, BAND, W), BF16),
            pltpu.SemaphoreType.DMA((BLOCKS // 4,)),
        ],
        name="cost_volume",
        cost_estimate=pl.CostEstimate(flops=5000000000, bytes_accessed=4500000, transcendentals=0),
        compiler_params=pltpu.CompilerParams(vmem_limit_bytes=24 * 1024 * 1024),
    )(table, floats, weights, pictures, *sums)


def all_of_it(table, floats, weights, pair, before, after, far):
    sums = early_sums(table, floats, weights, pair)
    pictures = jnp.concatenate([after, far[:1], before], axis=0)
    return cost_volume(table, floats, weights, pictures, sums)


def from_camera(value, source_of):
    return lax.ppermute(value, "cam", [(source_of(to) % CAMS, to) for to in range(CAMS)])


def on_device(
    images, neighbor_ids, neighbor_count, offsets, w_first, w_second, kernel_one, kernel_two, biases
):
    pair = jnp.concatenate([images, from_camera(images, lambda to: to ^ 1)], axis=0)
    ends = lax.axis_size("rows") - 1
    over = lax.ppermute(pair, "rows", [(i, i + 1) for i in range(ends)])
    under = lax.ppermute(pair, "rows", [(i + 1, i) for i in range(ends)])
    pair = jnp.concatenate([over[:, :, 4:], pair, under[:, :, :4]], axis=2)
    after = from_camera(pair, lambda to: to + 2)
    before = from_camera(pair, lambda to: to - 2)
    far = from_camera(pair, lambda to: to - 3 if to % 2 == 0 else to + 3)
    place = jnp.stack([lax.axis_index("cam"), lax.axis_index("rows") * BAND]).astype(jnp.int32)
    table = jnp.concatenate([place, neighbor_ids[0], offsets[0], neighbor_count])
    floats = jnp.concatenate([kernel_one, kernel_two, biases])
    weights = jnp.concatenate([w_second, jnp.pad(w_first.T, ((0, 5), (0, 0)))], axis=0)
    return all_of_it(table, floats, weights, pair, before, after, far)


def solution(mesh):
    in_specs = (
        P("cam", None, "rows", None),
        P("cam", None),
        P("cam"),
        P("cam", None),
        P(),
        P(),
        P(),
        P(),
        P(),
    )
    out_specs = P("cam", None, "rows", None)
    return jax.shard_map(
        on_device, mesh=mesh, in_specs=in_specs, out_specs=out_specs, check_vma=False
    )
```
